32 devices in a mesh: dp: 8 (over z, x), tensor: 4 (over y, core).
Axes of the slice: x: 2, y: 2, z: 4, core: 2. Of those that a mesh axis runs over, the one named last changes fastest.
Arguments:
- gradients: float32 [8, 16, 3, 28672], P('dp', None, None, 'tensor'), may hold values from -131072 to 131072
- token_counts: int32 [8, 3], P('dp'), may hold values from 512 to 6143
- modality: int32 [8], P('dp'), may hold values from 0 to 2
- loss_weight: float32 [3], replicated, may hold values from 0.5 to 2
- master: float32 [16, 3, 28672], P('dp', None, 'tensor'), may hold values from -6 to 6
- moment_one: float32 [16, 3, 28672], P('dp', None, 'tensor'), may hold values from -6 to 6
- moment_two: float32 [16, 3, 28672], P('dp', None, 'tensor'), may hold values from 0.05 to 2
Outputs:
- new_master: float32 [16, 3, 28672], P('dp', None, 'tensor')
- new_moment_one: float32 [16, 3, 28672], P('dp', None, 'tensor')
- new_moment_two: float32 [16, 3, 28672], P('dp', None, 'tensor')
- working_weights: bfloat16 [16, 3, 28672], P(None, None, 'tensor')
The draws below stay inside these ranges and needn't reach their ends.
Inputs may be any that keep to these rules, and one draw needn't show every extreme that they name: `modality`: 0 is text, 1 image, 2 audio.
All inputs are finite; a program needn't handle non-finite values.
Results may differ from the reference program's by a relative error of at most 0.001.
Values may be sent and summed in bfloat16 or wider, within the bound.
A program may use at most 128 MiB of HBM per device.

```python
import math
import jax
import jax.numpy as jnp
from jax import lax

FF = 28672
ROWS_DEV = 2
ROWS = 16
N_DP = 8


def draw_token_counts(key, part):
    replicas = ROWS // ROWS_DEV
    ranks = jnp.arange(replicas, dtype=jnp.int32)
    lowest = 512 + 1024 * ranks // max(replicas - 1, 1)
    counts = jax.random.randint(key, (replicas, 3), lowest[:, None], 4 * lowest[:, None], dtype=jnp.int32)
    counts = counts.at[0, 0].set(512)
    counts = counts.at[replicas - 1, 1].set(6143)
    return counts


def plant(entries, rng, low, top_value):
    longest = entries.shape.index(max(entries.shape))
    spots = []
    for shift in (0, 1):
        where = [jax.random.randint(jax.random.fold_in(rng, axis), (), 0, length) for axis, length in enumerate(entries.shape)]
        where[longest] = (where[longest] + shift) % entries.shape[longest]
        spots.append(tuple(where))
    return entries.at[spots[0]].set(low).at[spots[1]].set(top_value)


def raised(drawn, key, source, target, blocks, factor):
    owner, partner = [(jnp.arange(drawn.shape[dim]) // (drawn.shape[dim] // blocks)).reshape([-1 if axis == dim else 1 for axis in range(drawn.ndim)]) for dim in (source, target)]
    chosen = jax.random.permutation(key, blocks)[partner]
    strong = (owner == chosen) | (owner == (partner + blocks // 2) % blocks)
    return jnp.where(strong, factor * drawn, drawn)


def levels(rng, shape, shards, least, high):
    def one(axis_at, shards_of):
        draws = jax.random.uniform(jax.random.fold_in(jax.random.fold_in(rng, 6), axis_at), (shards_of,), jnp.float32, least / len(shards), high / len(shards))
        return jnp.repeat(jnp.exp(draws), shape[axis_at] // shards_of).reshape((-1,) + (1,) * (len(shape) - axis_at - 1))

    loudness = one(*shards[0])
    for cut in shards[1:]:
        loudness = loudness * one(*cut)
    return loudness


def centred(key, extent, width, reach, cuts=(), kind=jnp.bfloat16):
    level = levels(key, extent, cuts, -0.22, 0.18) if cuts else 1.0
    values = jax.random.normal(key, extent, jnp.float32) * width * level
    return jnp.minimum(jnp.maximum(values, -reach), reach).astype(kind)


def gaussian_with(own_key, dims, scale, most, pieces, heavy, held_as=jnp.bfloat16):
    values = scale * jax.random.normal(own_key, dims, jnp.float32)
    if pieces:
        values = values * levels(own_key, dims, pieces, -0.22, 0.18)
    return jnp.clip(raised(values, jax.random.fold_in(own_key, 3), *heavy), -most, most).astype(held_as)


def setup_inputs(seed: int = 0) -> dict:
    key_of = jax.random.split(jax.random.key(seed), 8)
    gradients = gaussian_with(key_of[0], (N_DP, ROWS, 3, FF), (1920 * N_DP), 131072.0, ((0, 8), (3, 4)), (0, 1, 8, 2.0), jnp.float32)
    token_counts = draw_token_counts(jax.random.fold_in(key_of[7], 71), 0)
    modality = plant(jax.random.randint(key_of[2], (N_DP,), 0, 3), jax.random.fold_in(key_of[2], 1), 0, 2).astype(jnp.int32)
    loss_weight = jnp.clip(jnp.exp(jax.random.uniform(key_of[3], (3,), jnp.float32, math.log(0.5), math.log(2.0))), 0.5, 2.0)
    master = centred(key_of[4], (ROWS, 3, FF), 1.0, 6.0, ((0, 8), (2, 4)), jnp.float32)
    moment_one = centred(key_of[5], (ROWS, 3, FF), 0.5, 6.0, ((0, 8), (2, 4)), jnp.float32)
    moment_two = jnp.clip(jnp.exp(math.log(2.0) - 3.6888794 * jax.random.uniform(key_of[6], (ROWS, 3, FF), jnp.float32) ** levels(key_of[6], (ROWS, 3, FF), ((0, 8), (2, 4)), -0.2, 0.2)), 0.05, 2.0)
    return dict(gradients=gradients, token_counts=token_counts, modality=modality, loss_weight=loss_weight, master=master, moment_one=moment_one, moment_two=moment_two)


beta_one = 0.9
beta_two = 0.95
bias_one = 1.0 - 0.9 ** 10
bias_two = 1.0 - 0.95 ** 10
epsilon = 1e-08
learn_rate = 0.01
decay_rate = 0.1

def adam_update(grad_sum, first, second, weights):
    first_new = beta_one * first + (1.0 - beta_one) * grad_sum
    second_new = beta_two * second + (1.0 - beta_two) * grad_sum * grad_sum
    step_size = first_new / bias_one / (jnp.sqrt(second_new / bias_two) + epsilon)
    weights_new = weights - learn_rate * (step_size + decay_rate * weights)
    return (weights_new, first_new, second_new)

def reference(gradients, token_counts, modality, loss_weight, master, moment_one, moment_two):
    totals = lax.optimization_barrier(jnp.sum(token_counts, axis=0)).astype(jnp.float32)
    ratios = loss_weight / totals
    picked = (modality[:, None] == jnp.arange(3, dtype=jnp.int32)[None, :]).astype(jnp.float32)
    scales = lax.optimization_barrier(jnp.sum(picked * ratios[None, :], axis=1))

    def accumulate(running, paired):
        return (running + paired[0] * paired[1], None)
    grad_sum, ignored = lax.scan(accumulate, jnp.zeros(gradients.shape[1:], jnp.float32), (gradients, scales))
    weights_new, first_new, second_new = adam_update(grad_sum, moment_one, moment_two, master)
    return (weights_new, first_new, second_new, weights_new.astype(jnp.bfloat16))
```

```python
import functools

import jax
import jax.numpy as jnp
from jax import lax
from jax.experimental import pallas as pl
from jax.experimental.pallas import tpu as pltpu
from jax.sharding import PartitionSpec as P

beta_one = 0.9
beta_two = 0.95
bias_one = 1.0 - 0.9**10
bias_two = 1.0 - 0.95**10
epsilon = 1e-08
learn_rate = 0.01
decay_rate = 0.1

WIRE = jnp.float32


def adam_update(grad_sum, first, second, weights):
    first_new = beta_one * first + (1.0 - beta_one) * grad_sum
    second_new = beta_two * second + (1.0 - beta_two) * grad_sum * grad_sum
    step_size = first_new / bias_one / (jnp.sqrt(second_new / bias_two) + epsilon)
    weights_new = weights - learn_rate * (step_size + decay_rate * weights)
    return (weights_new, first_new, second_new)


def kernel(
    n, rows_dev, mats, pieces, width,
    g_ref, counts_ref, modality_ref, weight_ref, master_ref, one_ref, two_ref,
    master_out, one_out, two_out, gathered,
    info_send, info, packed, send_a, recv_a, send_b, recv_b, own, state,
    si, ri, sa, ra, sb, rb, sc, rc, sd,
):
    half = n // 2
    me = lax.axis_index("dp")
    o, i = me // 2, me % 2
    mate = 2 * o + (1 - i)

    barrier = pltpu.get_barrier_semaphore()

    def greet(k, _):
        pl.semaphore_signal(
            barrier, inc=1, device_id={"dp": (me + k) % n}, device_id_type=pl.DeviceIdType.MESH
        )
        return 0

    lax.fori_loop(1, n, greet, 0)

    def pack(src, dst, first_row, m):
        for r in range(rows_dev):
            for p in range(pieces):
                row = r * pieces + p
                dst[row : row + 1, :] = src[pl.ds(first_row + r, 1), m, p * width : (p + 1) * width]

    def remote(src, dst, send, recv, target):
        return pltpu.make_async_remote_copy(
            src_ref=src,
            dst_ref=dst,
            send_sem=send,
            recv_sem=recv,
            device_id={"dp": target},
            device_id_type=pl.DeviceIdType.MESH,
        )

    g = g_ref.at[0]

    line = lax.broadcasted_iota(jnp.int32, info_send.shape, 0)
    told = jnp.where(line == 3, modality_ref[0], 0)
    for m in range(3):
        told = jnp.where(line == m, counts_ref[0, m], told)
    info_send[...] = told
    info[me] = told

    def copy_a(od, m):
        return remote(send_a.at[od, m], recv_a.at[od, m], sa.at[od, m], ra.at[od, m], mate)

    def fill_a(k, m):
        od = (o + 1 + k) % half
        d = 2 * od + (1 - i)
        pack(g, packed.at[d, m], d * rows_dev, m)
        send_a[od, m] = packed[d, m]

    fill_a(0, 0)
    pl.semaphore_wait(barrier, n - 1)
    copy_a((o + 1) % half, 0).start()

    def tell(k, _):
        remote(info_send, info.at[me], si.at[k], ri.at[me], (me + k) % n).start()
        return 0

    lax.fori_loop(1, n, tell, 0)

    for m in range(mats):
        def step_a(k, _, m=m):
            fill_a(k, m)
            copy_a((o + 1 + k) % half, m).start()
            return 0

        lax.fori_loop(1 if m == 0 else 0, half, step_a, 0)

    for m in range(mats):
        def keep(od, _, m=m):
            d = 2 * od + i
            pack(g, packed.at[d, m], d * rows_dev, m)
            return 0

        lax.fori_loop(0, half, keep, 0)

    def hear(k, _):
        source = (me + k) % n
        remote(info_send, info.at[source], si.at[k], ri.at[source], source).wait()
        return 0

    lax.fori_loop(1, n, hear, 0)

    totals = lax.fori_loop(1, n, lambda r, t: t + info[r], info[0])
    ratios = [weight_ref[m] / totals[m : m + 1].astype(jnp.float32) for m in range(3)]

    def scale_of(replica):
        kind = info[replica][3:4]
        picked = jnp.where(kind == 2, ratios[2], jnp.where(kind == 1, ratios[1], ratios[0]))
        return jnp.concatenate([picked] * (width // 128), axis=1)

    my_scale = scale_of(me)
    mate_scale = scale_of(mate)

    def copy_b(od, m):
        return remote(send_b.at[od, m], recv_b.at[o, m], sb.at[od, m], rb.at[o, m], 2 * od + i)

    def paired(od, m):
        copy_a(od, m).wait()
        return packed[2 * od + i, m] * my_scale + recv_a[od, m] * mate_scale

    def phase_b(m):
        def step(k, _):
            od = (o + 1 + k) % half
            send_b[od, m] = paired(od, m)
            copy_b(od, m).start()
            return 0

        lax.fori_loop(0, half - 1, step, 0)
        own[m] = paired(o, m)

    def copy_c(target, slot, m):
        return remote(gathered.at[me, m], gathered.at[me, m], sc.at[slot, m], rc.at[me, m], target)

    def finish(m):
        pack(master_ref, state.at[0, m], 0, m)
        pack(one_ref, state.at[1, m], 0, m)
        pack(two_ref, state.at[2, m], 0, m)

        def add(k, total):
            source = (o + k) % half
            pltpu.make_async_remote_copy(
                src_ref=send_b.at[source, m], dst_ref=recv_b.at[source, m],
                send_sem=sb.at[source, m], recv_sem=rb.at[source, m],
                device_id={"dp": mate}, device_id_type=pl.DeviceIdType.MESH,
            ).wait()
            return total + recv_b[source, m]

        summed = lax.fori_loop(1, half, add, own[m])
        weights_new, first_new, second_new = adam_update(summed, state[1, m], state[2, m], state[0, m])
        gathered[me, m] = weights_new.astype(jnp.bfloat16)
        copy_c(mate, 0, m).start()

        def spread(k, _):
            copy_c(2 * ((o + k) % half) + i, k, m).start()
            return 0

        lax.fori_loop(1, half, spread, 0)
        state[0, m] = weights_new
        state[1, m] = first_new
        state[2, m] = second_new
        for slot, out in enumerate((master_out, one_out, two_out)):
            for r in range(rows_dev):
                for p in range(pieces):
                    row = r * pieces + p
                    out[r : r + 1, m, p * width : (p + 1) * width] = state[slot, m, row : row + 1, :]

    def copy_d(od, m):
        d = 2 * od + i
        return remote(gathered.at[d, m], gathered.at[d, m], sd.at[od, m], rc.at[d, m], mate)

    def forward(m):
        def step(k, _):
            od = (o + k) % half
            d = 2 * od + i
            remote(gathered.at[d, m], gathered.at[d, m], sd.at[od, m], rc.at[d, m], mate).wait_recv()
            copy_d(od, m).start()
            return 0

        lax.fori_loop(1, half, step, 0)

    phase_b(0)
    for m in range(mats):
        if m + 1 < mats:
            phase_b(m + 1)
        finish(m)
        if m > 0:
            forward(m - 1)
    forward(mats - 1)

    for m in range(mats):
        def last(k, _, m=m):
            od = (o + k) % half
            copy_c(mate, k, m).wait_send()
            d = 2 * od + (1 - i)
            remote(gathered.at[d, m], gathered.at[d, m], sd.at[od, m], rc.at[d, m], mate).wait_recv()
            return 0

        lax.fori_loop(0, half, last, 0)

        def sent(k, _, m=m):
            copy_d((o + k) % half, m).wait_send()
            return 0

        lax.fori_loop(1, half, sent, 0)


def local(n, gradients, token_counts, modality, loss_weight, master, moment_one, moment_two):
    rows_dev, mats, columns = master.shape
    half = n // 2
    pieces = 8
    width = columns // pieces
    lines = rows_dev * pieces
    vmem = pl.BlockSpec(memory_space=pltpu.VMEM)
    smem = pl.BlockSpec(memory_space=pltpu.SMEM)
    dma = pltpu.SemaphoreType.DMA
    state_shape = jax.ShapeDtypeStruct(master.shape, jnp.float32)
    weights_new, first_new, second_new, gathered = pl.pallas_call(
        functools.partial(kernel, n, rows_dev, mats, pieces, width),
        out_shape=(
            state_shape,
            state_shape,
            state_shape,
            jax.ShapeDtypeStruct((n, mats, lines, width), jnp.bfloat16),
        ),
        in_specs=[vmem, smem, smem, smem, vmem, vmem, vmem],
        out_specs=(vmem,) * 4,
        scratch_shapes=[
            pltpu.VMEM((8, 128), jnp.int32),
            pltpu.VMEM((n, 8, 128), jnp.int32),
            pltpu.VMEM((n, mats, lines, width), jnp.float32),
            pltpu.VMEM((half, mats, lines, width), WIRE),
            pltpu.VMEM((half, mats, lines, width), WIRE),
            pltpu.VMEM((half, mats, lines, width), WIRE),
            pltpu.VMEM((half, mats, lines, width), WIRE),
            pltpu.VMEM((mats, lines, width), jnp.float32),
            pltpu.VMEM((3, mats, lines, width), jnp.float32),
            dma((n,)),
            dma((n,)),
            dma((half, mats)),
            dma((half, mats)),
            dma((half, mats)),
            dma((half, mats)),
            dma((half, mats)),
            dma((n, mats)),
            dma((half, mats)),
        ],
        compiler_params=pltpu.CompilerParams(
            collective_id=0, has_side_effects=True, vmem_limit_bytes=60 * 2**20
        ),
    )(gradients, token_counts, modality, loss_weight, master, moment_one, moment_two)
    working = gathered.reshape(n, mats, rows_dev, columns).transpose(0, 2, 1, 3)
    return (weights_new, first_new, second_new, working.reshape(n * rows_dev, mats, columns))


def solution(mesh):
    placed = (
        P("dp", None, None, "tensor"),
        P("dp", None),
        P("dp"),
        P(),
        P("dp", None, "tensor"),
        P("dp", None, "tensor"),
        P("dp", None, "tensor"),
    )
    return jax.shard_map(
        functools.partial(local, mesh.shape["dp"]),
        mesh=mesh,
        in_specs=placed,
        out_specs=(
            P("dp", None, "tensor"),
            P("dp", None, "tensor"),
            P("dp", None, "tensor"),
            P(None, None, "tensor"),
        ),
        check_vma=False,
    )
```

```python
import functools

import jax
import jax.numpy as jnp
from jax import lax
from jax.experimental import pallas as pl
from jax.experimental.pallas import tpu as pltpu
from jax.sharding import PartitionSpec as P

beta_one = 0.9
beta_two = 0.95
bias_one = 1.0 - 0.9**10
bias_two = 1.0 - 0.95**10
epsilon = 1e-08
learn_rate = 0.01
decay_rate = 0.1

WIRE = jnp.float32


def adam_update(grad_sum, first, second, weights):
    first_new = beta_one * first + (1.0 - beta_one) * grad_sum
    second_new = beta_two * second + (1.0 - beta_two) * grad_sum * grad_sum
    step_size = first_new / bias_one / (jnp.sqrt(second_new / bias_two) + epsilon)
    weights_new = weights - learn_rate * (step_size + decay_rate * weights)
    return (weights_new, first_new, second_new)


def kernel(
    n, rows_dev, mats, pieces, width,
    g_ref, counts_ref, modality_ref, weight_ref, master_ref, one_ref, two_ref,
    master_out, one_out, two_out, working,
    info_send, info, gathered, spread_out, kept, send_a, recv_a, send_b, recv_b, own, state,
    si, ri, sa, ra, sb, rb, sc, rc, sd,
):
    half = n // 2
    me = lax.axis_index("dp")
    o, i = me // 2, me % 2
    mate = 2 * o + (1 - i)

    barrier = pltpu.get_barrier_semaphore()

    def greet(k, _):
        pl.semaphore_signal(
            barrier, inc=1, device_id={"dp": (me + k) % n}, device_id_type=pl.DeviceIdType.MESH
        )
        return 0

    lax.fori_loop(1, n, greet, 0)

    def pack(src, dst, first_row, m):
        for r in range(rows_dev):
            for p in range(pieces):
                row = r * pieces + p
                dst[row : row + 1, :] = src[m, pl.ds(first_row + r, 1), p * width : (p + 1) * width]

    def remote(src, dst, send, recv, target):
        return pltpu.make_async_remote_copy(
            src_ref=src,
            dst_ref=dst,
            send_sem=send,
            recv_sem=recv,
            device_id={"dp": target},
            device_id_type=pl.DeviceIdType.MESH,
        )

    g = g_ref.at[0]

    line = lax.broadcasted_iota(jnp.int32, info_send.shape, 0)
    told = jnp.where(line == 3, modality_ref[0], 0)
    for m in range(3):
        told = jnp.where(line == m, counts_ref[0, m], told)
    info_send[...] = told
    info[me] = told

    def copy_a(od, m):
        return remote(send_a.at[od, m], recv_a.at[od, m], sa.at[od, m], ra.at[od, m], mate)

    def fill_a(k, m):
        od = (o + 1 + k) % half
        d = 2 * od + (1 - i)
        pack(g, send_a.at[od, m], d * rows_dev, m)

    fill_a(0, 0)
    pl.semaphore_wait(barrier, n - 1)
    copy_a((o + 1) % half, 0).start()

    def tell(k, _):
        remote(info_send, info.at[me], si.at[k], ri.at[me], (me + k) % n).start()
        return 0

    lax.fori_loop(1, n, tell, 0)

    for m in range(mats):
        def step_a(k, _, m=m):
            fill_a(k, m)
            copy_a((o + 1 + k) % half, m).start()
            return 0

        lax.fori_loop(1 if m == 0 else 0, half, step_a, 0)

    for m in range(mats):
        def keep(od, _, m=m):
            pack(g, kept.at[od, m], (2 * od + i) * rows_dev, m)
            return 0

        lax.fori_loop(0, half, keep, 0)

    def hear(k, _):
        source = (me + k) % n
        remote(info_send, info.at[source], si.at[k], ri.at[source], source).wait()
        return 0

    lax.fori_loop(1, n, hear, 0)

    totals = lax.fori_loop(1, n, lambda r, t: t + info[r], info[0])
    ratios = [weight_ref[m] / totals[m : m + 1].astype(jnp.float32) for m in range(3)]

    def scale_of(replica):
        kind = info[replica][3:4]
        picked = jnp.where(kind == 2, ratios[2], jnp.where(kind == 1, ratios[1], ratios[0]))
        return jnp.concatenate([picked] * (width // 128), axis=1)

    my_scale = scale_of(me)
    mate_scale = scale_of(mate)

    def copy_b(od, m):
        return remote(send_b.at[od, m], recv_b.at[o, m], sb.at[od, m], rb.at[o, m], 2 * od + i)

    def paired(od, m):
        copy_a(od, m).wait()
        return kept[od, m] * my_scale + recv_a[od, m] * mate_scale

    def phase_b(m):
        def step(k, _):
            od = (o + 1 + k) % half
            send_b[od, m] = paired(od, m)
            copy_b(od, m).start()
            return 0

        lax.fori_loop(0, half - 1, step, 0)
        own[m] = paired(o, m)

    def copy_c(target, slot, m):
        return remote(gathered.at[me, m], gathered.at[me, m], sc.at[slot, m], rc.at[me, m], target)

    def finish(m):
        pack(master_ref, state.at[0, m], 0, m)
        pack(one_ref, state.at[1, m], 0, m)
        pack(two_ref, state.at[2, m], 0, m)

        def add(k, total):
            source = (o + k) % half
            pltpu.make_async_remote_copy(
                src_ref=send_b.at[source, m], dst_ref=recv_b.at[source, m],
                send_sem=sb.at[source, m], recv_sem=rb.at[source, m],
                device_id={"dp": mate}, device_id_type=pl.DeviceIdType.MESH,
            ).wait()
            return total + recv_b[source, m]

        summed = lax.fori_loop(1, half, add, own[m])
        weights_new, first_new, second_new = adam_update(summed, state[1, m], state[2, m], state[0, m])
        gathered[me, m] = weights_new.astype(jnp.bfloat16)
        copy_c(mate, 0, m).start()

        def spread(k, _):
            copy_c(2 * ((o + k) % half) + i, k, m).start()
            return 0

        lax.fori_loop(1, half, spread, 0)
        state[0, m] = weights_new
        state[1, m] = first_new
        state[2, m] = second_new
        for slot, out in enumerate((master_out, one_out, two_out)):
            for r in range(rows_dev):
                for p in range(pieces):
                    row = r * pieces + p
                    out[m, r : r + 1, p * width : (p + 1) * width] = state[slot, m, row : row + 1, :]

    def copy_d(od, m):
        d = 2 * od + i
        return remote(gathered.at[d, m], gathered.at[d, m], sd.at[od, m], rc.at[d, m], mate)

    def forward(m):
        def step(k, _):
            od = (o + k) % half
            d = 2 * od + i
            remote(gathered.at[d, m], gathered.at[d, m], sd.at[od, m], rc.at[d, m], mate).wait_recv()
            copy_d(od, m).start()
            return 0

        lax.fori_loop(1, half, step, 0)

    def unpack(d, m):
        block = gathered[d, m].astype(jnp.float32)
        for r in range(rows_dev):
            for p in range(pieces):
                row = r * pieces + p
                spread_out[pl.ds(d * rows_dev + r, 1), p * width : (p + 1) * width] = block[row : row + 1, :]

    phase_b(0)
    for m in range(mats):
        if m + 1 < mats:
            phase_b(m + 1)
        finish(m)
        if m > 0:
            forward(m - 1)
    forward(mats - 1)

    for m in range(mats):
        def held(od, _, m=m):
            unpack(2 * od + i, m)
            return 0

        lax.fori_loop(0, half, held, 0)

        def last(k, _, m=m):
            od = (o + k) % half
            d = 2 * od + (1 - i)
            remote(gathered.at[d, m], gathered.at[d, m], sd.at[od, m], rc.at[d, m], mate).wait_recv()
            unpack(d, m)
            return 0

        lax.fori_loop(0, half, last, 0)
        working[m] = spread_out[...].astype(jnp.bfloat16)

    for m in range(mats):
        def given(k, _, m=m):
            copy_c(mate, k, m).wait_send()
            return 0

        lax.fori_loop(0, half, given, 0)

        def sent(k, _, m=m):
            copy_d((o + k) % half, m).wait_send()
            return 0

        lax.fori_loop(1, half, sent, 0)


def local(n, gradients, token_counts, modality, loss_weight, master, moment_one, moment_two):
    rows_dev, mats, columns = master.shape
    half = n // 2
    pieces = 8
    width = columns // pieces
    lines = rows_dev * pieces
    vmem = pl.BlockSpec(memory_space=pltpu.VMEM)
    smem = pl.BlockSpec(memory_space=pltpu.SMEM)
    dma = pltpu.SemaphoreType.DMA
    state_shape = jax.ShapeDtypeStruct((mats, rows_dev, columns), jnp.float32)
    weights_new, first_new, second_new, working = pl.pallas_call(
        functools.partial(kernel, n, rows_dev, mats, pieces, width),
        out_shape=(
            state_shape,
            state_shape,
            state_shape,
            jax.ShapeDtypeStruct((mats, n * rows_dev, columns), jnp.bfloat16),
        ),
        in_specs=[vmem, smem, smem, smem, vmem, vmem, vmem],
        out_specs=(vmem,) * 4,
        scratch_shapes=[
            pltpu.VMEM((8, 128), jnp.int32),
            pltpu.VMEM((n, 8, 128), jnp.int32),
            pltpu.VMEM((n, mats, lines, width), jnp.bfloat16),
            pltpu.VMEM((n * rows_dev, columns), jnp.float32),
            pltpu.VMEM((half, mats, lines, width), jnp.float32),
            pltpu.VMEM((half, mats, lines, width), WIRE),
            pltpu.VMEM((half, mats, lines, width), WIRE),
            pltpu.VMEM((half, mats, lines, width), WIRE),
            pltpu.VMEM((half, mats, lines, width), WIRE),
            pltpu.VMEM((mats, lines, width), jnp.float32),
            pltpu.VMEM((3, mats, lines, width), jnp.float32),
            dma((n,)),
            dma((n,)),
            dma((half, mats)),
            dma((half, mats)),
            dma((half, mats)),
            dma((half, mats)),
            dma((half, mats)),
            dma((n, mats)),
            dma((half, mats)),
        ],
        compiler_params=pltpu.CompilerParams(
            collective_id=0, has_side_effects=True, vmem_limit_bytes=60 * 2**20
        ),
    )(
        gradients.transpose(0, 2, 1, 3), token_counts, modality, loss_weight,
        master.transpose(1, 0, 2), moment_one.transpose(1, 0, 2), moment_two.transpose(1, 0, 2),
    )
    return tuple(a.transpose(1, 0, 2) for a in (weights_new, first_new, second_new, working))


def solution(mesh):
    placed = (
        P("dp", None, None, "tensor"),
        P("dp", None),
        P("dp"),
        P(),
        P("dp", None, "tensor"),
        P("dp", None, "tensor"),
        P("dp", None, "tensor"),
    )
    return jax.shard_map(
        functools.partial(local, mesh.shape["dp"]),
        mesh=mesh,
        in_specs=placed,
        out_specs=(
            P("dp", None, "tensor"),
            P("dp", None, "tensor"),
            P("dp", None, "tensor"),
            P(None, None, "tensor"),
        ),
        check_vma=False,
    )
```

```python
import functools

import jax
import jax.numpy as jnp
from jax import lax
from jax.experimental import pallas as pl
from jax.experimental.pallas import tpu as pltpu
from jax.sharding import PartitionSpec as P

beta_one = 0.9
beta_two = 0.95
bias_one = 1.0 - 0.9**10
bias_two = 1.0 - 0.95**10
epsilon = 1e-08
learn_rate = 0.01
decay_rate = 0.1

WIRE = jnp.float32


def adam_update(grad_sum, first, second, weights):
    first_new = beta_one * first + (1.0 - beta_one) * grad_sum
    second_new = beta_two * second + (1.0 - beta_two) * grad_sum * grad_sum
    step_size = first_new / bias_one / (jnp.sqrt(second_new / bias_two) + epsilon)
    weights_new = weights - learn_rate * (step_size + decay_rate * weights)
    return (weights_new, first_new, second_new)


def kernel(
    n, rows_dev, mats, pieces, width,
    g_ref, counts_ref, modality_ref, weight_ref, master_ref, one_ref, two_ref,
    master_out, one_out, two_out, working,
    info_send, info, gathered, spread_out, kept, send_a, recv_a, send_b, recv_b, own, state,
    si, ri, sa, ra, sb, rb, sc, rc, sd,
):
    half = n // 2
    me = lax.axis_index("dp")
    o, i = me // 2, me % 2
    mate = 2 * o + (1 - i)

    barrier = pltpu.get_barrier_semaphore()

    def greet(k, _):
        pl.semaphore_signal(
            barrier, inc=1, device_id={"dp": (me + k) % n}, device_id_type=pl.DeviceIdType.MESH
        )
        return 0

    lax.fori_loop(1, n, greet, 0)

    cut = (width // 128 + 1) // 2 * 128
    chunks = [(m, lo, hi) for m in range(mats) for lo, hi in ((0, cut), (cut, width))]

    def part(ref, index, c):
        m, lo, hi = chunks[c]
        return ref.at[index, m, :, lo:hi]

    def pack(src, dst, first_row, c):
        m, lo, hi = chunks[c]
        for r in range(rows_dev):
            for p in range(pieces):
                row = r * pieces + p
                dst[row : row + 1, lo:hi] = src[m, pl.ds(first_row + r, 1), p * width + lo : p * width + hi]

    def remote(src, dst, send, recv, target):
        return pltpu.make_async_remote_copy(
            src_ref=src,
            dst_ref=dst,
            send_sem=send,
            recv_sem=recv,
            device_id={"dp": target},
            device_id_type=pl.DeviceIdType.MESH,
        )

    g = g_ref.at[0]

    line = lax.broadcasted_iota(jnp.int32, info_send.shape, 0)
    told = jnp.where(line == 3, modality_ref[0], 0)
    for m in range(3):
        told = jnp.where(line == m, counts_ref[0, m], told)
    info_send[...] = told
    info[me] = told

    def copy_a(od, m):
        return remote(part(send_a, od, m), part(recv_a, od, m), sa.at[od, m], ra.at[od, m], mate)

    def fill_a(k, m):
        od = (o + 1 + k) % half
        d = 2 * od + (1 - i)
        pack(g, send_a.at[od, chunks[m][0]], d * rows_dev, m)

    fill_a(0, 0)
    pl.semaphore_wait(barrier, n - 1)
    copy_a((o + 1) % half, 0).start()

    def tell(k, _):
        remote(info_send, info.at[me], si.at[k], ri.at[me], (me + k) % n).start()
        return 0

    lax.fori_loop(1, n, tell, 0)

    for m in range(len(chunks)):
        def step_a(k, _, m=m):
            fill_a(k, m)
            copy_a((o + 1 + k) % half, m).start()
            return 0

        lax.fori_loop(1 if m == 0 else 0, half, step_a, 0)

    for m in range(len(chunks)):
        def keep(od, _, m=m):
            pack(g, kept.at[od, chunks[m][0]], (2 * od + i) * rows_dev, m)
            return 0

        lax.fori_loop(0, half, keep, 0)

    def hear(k, _):
        source = (me + k) % n
        remote(info_send, info.at[source], si.at[k], ri.at[source], source).wait()
        return 0

    lax.fori_loop(1, n, hear, 0)

    totals = lax.fori_loop(1, n, lambda r, t: t + info[r], info[0])
    ratios = [weight_ref[m] / totals[m : m + 1].astype(jnp.float32) for m in range(3)]

    def scale_of(replica):
        kind = info[replica][3:4]
        picked = jnp.where(kind == 2, ratios[2], jnp.where(kind == 1, ratios[1], ratios[0]))
        return jnp.concatenate([picked] * (width // 128), axis=1)

    my_scale = scale_of(me)
    mate_scale = scale_of(mate)

    def copy_b(od, m):
        return remote(part(send_b, od, m), part(recv_b, o, m), sb.at[od, m], rb.at[o, m], 2 * od + i)

    def paired(od, m):
        copy_a(od, m).wait()
        mat, lo, hi = chunks[m]
        mine = kept[od, mat, :, lo:hi] * my_scale[:, lo:hi]
        return mine + recv_a[od, mat, :, lo:hi] * mate_scale[:, lo:hi]

    def phase_b(m):
        mat, lo, hi = chunks[m]

        def step(k, _):
            od = (o + 1 + k) % half
            send_b[od, mat, :, lo:hi] = paired(od, m)
            copy_b(od, m).start()
            return 0

        lax.fori_loop(0, half - 1, step, 0)
        own[mat, :, lo:hi] = paired(o, m)

    def copy_c(target, slot, m):
        return remote(part(gathered, me, m), part(gathered, me, m), sc.at[slot, m], rc.at[me, m], target)

    def finish(m):
        mat, lo, hi = chunks[m]
        pack(master_ref, state.at[0, chunks[m][0]], 0, m)
        pack(one_ref, state.at[1, chunks[m][0]], 0, m)
        pack(two_ref, state.at[2, chunks[m][0]], 0, m)

        def add(k, total):
            source = (o + k) % half
            pltpu.make_async_remote_copy(
                src_ref=part(send_b, source, m), dst_ref=part(recv_b, source, m),
                send_sem=sb.at[source, m], recv_sem=rb.at[source, m],
                device_id={"dp": mate}, device_id_type=pl.DeviceIdType.MESH,
            ).wait()
            return total + recv_b[source, mat, :, lo:hi]

        summed = lax.fori_loop(1, half, add, own[mat, :, lo:hi])
        weights_new, first_new, second_new = adam_update(summed, state[1, mat, :, lo:hi], state[2, mat, :, lo:hi], state[0, mat, :, lo:hi])
        gathered[me, mat, :, lo:hi] = weights_new.astype(jnp.bfloat16)
        copy_c(mate, 0, m).start()

        def spread(k, _):
            copy_c(2 * ((o + k) % half) + i, k, m).start()
            return 0

        lax.fori_loop(1, half, spread, 0)
        state[0, mat, :, lo:hi] = weights_new
        state[1, mat, :, lo:hi] = first_new
        state[2, mat, :, lo:hi] = second_new
        for slot, out in enumerate((master_out, one_out, two_out)):
            for r in range(rows_dev):
                for p in range(pieces):
                    row = r * pieces + p
                    out[mat, r : r + 1, p * width + lo : p * width + hi] = state[slot, mat, row : row + 1, lo:hi]

    def copy_d(od, m):
        d = 2 * od + i
        return remote(part(gathered, d, m), part(gathered, d, m), sd.at[od, m], rc.at[d, m], mate)

    def forward(m):
        def step(k, _):
            od = (o + k) % half
            d = 2 * od + i
            remote(part(gathered, d, m), part(gathered, d, m), sd.at[od, m], rc.at[d, m], mate).wait_recv()
            copy_d(od, m).start()
            return 0

        lax.fori_loop(1, half, step, 0)

    def unpack(d, m):
        mat, lo, hi = chunks[m]
        block = gathered[d, mat, :, lo:hi].astype(jnp.float32)
        for r in range(rows_dev):
            for p in range(pieces):
                row = r * pieces + p
                spread_out[pl.ds(d * rows_dev + r, 1), p * width + lo : p * width + hi] = block[row : row + 1, :]

    phase_b(0)
    for m in range(len(chunks)):
        if m + 1 < len(chunks):
            phase_b(m + 1)
        finish(m)
        if m > 0:
            forward(m - 1)
    forward(len(chunks) - 1)

    for m in range(len(chunks)):
        def held(od, _, m=m):
            unpack(2 * od + i, m)
            return 0

        lax.fori_loop(0, half, held, 0)

        def last(k, _, m=m):
            od = (o + k) % half
            d = 2 * od + (1 - i)
            remote(part(gathered, d, m), part(gathered, d, m), sd.at[od, m], rc.at[d, m], mate).wait_recv()
            unpack(d, m)
            return 0

        lax.fori_loop(0, half, last, 0)
        mat, lo, hi = chunks[m]
        if hi == width:
            working[mat] = spread_out[...].astype(jnp.bfloat16)

    for m in range(len(chunks)):
        def given(k, _, m=m):
            copy_c(mate, k, m).wait_send()
            return 0

        lax.fori_loop(0, half, given, 0)

        def sent(k, _, m=m):
            copy_d((o + k) % half, m).wait_send()
            return 0

        lax.fori_loop(1, half, sent, 0)


def local(n, gradients, token_counts, modality, loss_weight, master, moment_one, moment_two):
    rows_dev, mats, columns = master.shape
    half = n // 2
    pieces = 8
    width = columns // pieces
    lines = rows_dev * pieces
    vmem = pl.BlockSpec(memory_space=pltpu.VMEM)
    smem = pl.BlockSpec(memory_space=pltpu.SMEM)
    dma = pltpu.SemaphoreType.DMA
    state_shape = jax.ShapeDtypeStruct((mats, rows_dev, columns), jnp.float32)
    weights_new, first_new, second_new, working = pl.pallas_call(
        functools.partial(kernel, n, rows_dev, mats, pieces, width),
        out_shape=(
            state_shape,
            state_shape,
            state_shape,
            jax.ShapeDtypeStruct((mats, n * rows_dev, columns), jnp.bfloat16),
        ),
        in_specs=[vmem, smem, smem, smem, vmem, vmem, vmem],
        out_specs=(vmem,) * 4,
        scratch_shapes=[
            pltpu.VMEM((8, 128), jnp.int32),
            pltpu.VMEM((n, 8, 128), jnp.int32),
            pltpu.VMEM((n, mats, lines, width), jnp.bfloat16),
            pltpu.VMEM((n * rows_dev, columns), jnp.float32),
            pltpu.VMEM((half, mats, lines, width), jnp.float32),
            pltpu.VMEM((half, mats, lines, width), WIRE),
            pltpu.VMEM((half, mats, lines, width), WIRE),
            pltpu.VMEM((half, mats, lines, width), WIRE),
            pltpu.VMEM((half, mats, lines, width), WIRE),
            pltpu.VMEM((mats, lines, width), jnp.float32),
            pltpu.VMEM((3, mats, lines, width), jnp.float32),
            dma((n,)),
            dma((n,)),
            dma((half, 2 * mats)),
            dma((half, 2 * mats)),
            dma((half, 2 * mats)),
            dma((half, 2 * mats)),
            dma((half, 2 * mats)),
            dma((n, 2 * mats)),
            dma((half, 2 * mats)),
        ],
        compiler_params=pltpu.CompilerParams(
            collective_id=0, has_side_effects=True, vmem_limit_bytes=60 * 2**20
        ),
    )(
        gradients.transpose(0, 2, 1, 3), token_counts, modality, loss_weight,
        master.transpose(1, 0, 2), moment_one.transpose(1, 0, 2), moment_two.transpose(1, 0, 2),
    )
    return tuple(a.transpose(1, 0, 2) for a in (weights_new, first_new, second_new, working))


def solution(mesh):
    placed = (
        P("dp", None, None, "tensor"),
        P("dp", None),
        P("dp"),
        P(),
        P("dp", None, "tensor"),
        P("dp", None, "tensor"),
        P("dp", None, "tensor"),
    )
    return jax.shard_map(
        functools.partial(local, mesh.shape["dp"]),
        mesh=mesh,
        in_specs=placed,
        out_specs=(
            P("dp", None, "tensor"),
            P("dp", None, "tensor"),
            P("dp", None, "tensor"),
            P(None, None, "tensor"),
        ),
        check_vma=False,
    )
```

```python
import functools

import jax
import jax.numpy as jnp
from jax import lax
from jax.experimental import pallas as pl
from jax.experimental.pallas import tpu as pltpu
from jax.sharding import PartitionSpec as P

beta_one = 0.9
beta_two = 0.95
bias_one = 1.0 - 0.9**10
bias_two = 1.0 - 0.95**10
epsilon = 1e-08
learn_rate = 0.01
decay_rate = 0.1

WIRE = jnp.float32


def adam_update(grad_sum, first, second, weights):
    first_new = beta_one * first + (1.0 - beta_one) * grad_sum
    second_new = beta_two * second + (1.0 - beta_two) * grad_sum * grad_sum
    step_size = first_new / bias_one / (jnp.sqrt(second_new / bias_two) + epsilon)
    weights_new = weights - learn_rate * (step_size + decay_rate * weights)
    return (weights_new, first_new, second_new)


def kernel(
    n, rows_dev, mats, pieces, width,
    g_ref, counts_ref, modality_ref, weight_ref, master_ref, one_ref, two_ref,
    master_out, one_out, two_out, working,
    info_send, info, gathered, spread_out, kept, send_a, recv_a, send_b, recv_b, own, state,
    si, ri, sa, ra, sb, rb, sc, rc, sd,
):
    half = n // 2
    me = lax.axis_index("dp")
    o, i = me // 2, me % 2
    mate = 2 * o + (1 - i)

    barrier = pltpu.get_barrier_semaphore()

    def greet(k, _):
        pl.semaphore_signal(
            barrier, inc=1, device_id={"dp": (me + k) % n}, device_id_type=pl.DeviceIdType.MESH
        )
        return 0

    lax.fori_loop(1, n, greet, 0)

    def pack(src, dst, first_row, m):
        for r in range(rows_dev):
            for p in range(pieces):
                row = r * pieces + p
                dst[row : row + 1, :] = src[m, pl.ds(first_row + r, 1), p * width : (p + 1) * width]

    def remote(src, dst, send, recv, target):
        return pltpu.make_async_remote_copy(
            src_ref=src,
            dst_ref=dst,
            send_sem=send,
            recv_sem=recv,
            device_id={"dp": target},
            device_id_type=pl.DeviceIdType.MESH,
        )

    g = g_ref.at[0]

    line = lax.broadcasted_iota(jnp.int32, info_send.shape, 0)
    told = jnp.where(line == 3, modality_ref[0], 0)
    for m in range(3):
        told = jnp.where(line == m, counts_ref[0, m], told)
    info_send[...] = told
    info[me] = told

    def copy_a(od, m):
        return remote(send_a.at[od, m], recv_a.at[od, m], sa.at[od, m], ra.at[od, m], mate)

    def fill_a(k, m):
        od = (o + 1 + k) % half
        d = 2 * od + (1 - i)
        pack(g, send_a.at[od, m], d * rows_dev, m)

    fill_a(0, 0)
    pl.semaphore_wait(barrier, n - 1)
    copy_a((o + 1) % half, 0).start()

    def tell(k, _):
        remote(info_send, info.at[me], si.at[k], ri.at[me], (me + k) % n).start()
        return 0

    lax.fori_loop(1, n, tell, 0)

    for m in range(mats):
        def step_a(k, _, m=m):
            fill_a(k, m)
            copy_a((o + 1 + k) % half, m).start()
            return 0

        lax.fori_loop(1 if m == 0 else 0, half, step_a, 0)

    for m in range(mats):
        def keep(od, _, m=m):
            pack(g, kept.at[od, m], (2 * od + i) * rows_dev, m)
            return 0

        lax.fori_loop(0, half, keep, 0)
        pack(master_ref, state.at[0, m], 0, m)
        pack(one_ref, state.at[1, m], 0, m)
        pack(two_ref, state.at[2, m], 0, m)

    def hear(k, _):
        source = (me + k) % n
        remote(info_send, info.at[source], si.at[k], ri.at[source], source).wait()
        return 0

    lax.fori_loop(1, n, hear, 0)

    totals = lax.fori_loop(1, n, lambda r, t: t + info[r], info[0])
    ratios = [weight_ref[m] / totals[m : m + 1].astype(jnp.float32) for m in range(3)]

    def scale_of(replica):
        kind = info[replica][3:4]
        picked = jnp.where(kind == 2, ratios[2], jnp.where(kind == 1, ratios[1], ratios[0]))
        return jnp.concatenate([picked] * (width // 128), axis=1)

    my_scale = scale_of(me)
    mate_scale = scale_of(mate)

    def copy_b(od, m):
        return remote(send_b.at[od, m], recv_b.at[o, m], sb.at[od, m], rb.at[o, m], 2 * od + i)

    def paired(od, m):
        copy_a(od, m).wait()
        return kept[od, m] * my_scale + recv_a[od, m] * mate_scale

    def phase_b(m):
        def step(k, _):
            od = (o + 1 + k) % half
            send_b[od, m] = paired(od, m)
            copy_b(od, m).start()
            return 0

        lax.fori_loop(0, half - 1, step, 0)
        own[m] = paired(o, m)

    def copy_c(target, slot, m):
        return remote(gathered.at[me, m], gathered.at[me, m], sc.at[slot, m], rc.at[me, m], target)

    def finish(m):
        def add(k, total):
            source = (o + k) % half
            pltpu.make_async_remote_copy(
                src_ref=send_b.at[source, m], dst_ref=recv_b.at[source, m],
                send_sem=sb.at[source, m], recv_sem=rb.at[source, m],
                device_id={"dp": mate}, device_id_type=pl.DeviceIdType.MESH,
            ).wait()
            return total + recv_b[source, m]

        summed = lax.fori_loop(1, half, add, own[m])
        weights_new, first_new, second_new = adam_update(summed, state[1, m], state[2, m], state[0, m])
        gathered[me, m] = weights_new.astype(jnp.bfloat16)
        copy_c(mate, 0, m).start()

        def spread(k, _):
            copy_c(2 * ((o + k) % half) + i, k, m).start()
            return 0

        lax.fori_loop(1, half, spread, 0)
        state[0, m] = weights_new
        state[1, m] = first_new
        state[2, m] = second_new

    def write_state(m):
        for slot, out in enumerate((master_out, one_out, two_out)):
            for r in range(rows_dev):
                for p in range(pieces):
                    row = r * pieces + p
                    out[m, r : r + 1, p * width : (p + 1) * width] = state[slot, m, row : row + 1, :]

    def copy_d(od, m):
        d = 2 * od + i
        return remote(gathered.at[d, m], gathered.at[d, m], sd.at[od, m], rc.at[d, m], mate)

    def forward(m):
        def step(k, _):
            od = (o + k) % half
            d = 2 * od + i
            remote(gathered.at[d, m], gathered.at[d, m], sd.at[od, m], rc.at[d, m], mate).wait_recv()
            copy_d(od, m).start()
            return 0

        lax.fori_loop(1, half, step, 0)

    def unpack(d, m):
        block = gathered[d, m].astype(jnp.float32)
        for r in range(rows_dev):
            for p in range(pieces):
                row = r * pieces + p
                spread_out[pl.ds(d * rows_dev + r, 1), p * width : (p + 1) * width] = block[row : row + 1, :]

    def collect(m):
        def held(od, _):
            unpack(2 * od + i, m)
            return 0

        lax.fori_loop(0, half, held, 0)

        def last(k, _):
            od = (o + k) % half
            d = 2 * od + (1 - i)
            remote(gathered.at[d, m], gathered.at[d, m], sd.at[od, m], rc.at[d, m], mate).wait_recv()
            unpack(d, m)
            return 0

        lax.fori_loop(0, half, last, 0)
        working[m] = spread_out[...].astype(jnp.bfloat16)

    phase_b(0)
    for m in range(mats):
        if m + 1 < mats:
            phase_b(m + 1)
        finish(m)
        if m > 0:
            forward(m - 1)
    forward(mats - 1)
    for m in range(mats):
        write_state(m)
    for m in range(mats):
        collect(m)

    for m in range(mats):
        def given(k, _, m=m):
            copy_c(mate, k, m).wait_send()
            return 0

        lax.fori_loop(0, half, given, 0)

        def sent(k, _, m=m):
            copy_d((o + k) % half, m).wait_send()
            return 0

        lax.fori_loop(1, half, sent, 0)


def local(n, gradients, token_counts, modality, loss_weight, master, moment_one, moment_two):
    rows_dev, mats, columns = master.shape
    half = n // 2
    pieces = 8
    width = columns // pieces
    lines = rows_dev * pieces
    vmem = pl.BlockSpec(memory_space=pltpu.VMEM)
    smem = pl.BlockSpec(memory_space=pltpu.SMEM)
    dma = pltpu.SemaphoreType.DMA
    state_shape = jax.ShapeDtypeStruct((mats, rows_dev, columns), jnp.float32)
    weights_new, first_new, second_new, working = pl.pallas_call(
        functools.partial(kernel, n, rows_dev, mats, pieces, width),
        out_shape=(
            state_shape,
            state_shape,
            state_shape,
            jax.ShapeDtypeStruct((mats, n * rows_dev, columns), jnp.bfloat16),
        ),
        in_specs=[vmem, smem, smem, smem, vmem, vmem, vmem],
        out_specs=(vmem,) * 4,
        scratch_shapes=[
            pltpu.VMEM((8, 128), jnp.int32),
            pltpu.VMEM((n, 8, 128), jnp.int32),
            pltpu.VMEM((n, mats, lines, width), jnp.bfloat16),
            pltpu.VMEM((n * rows_dev, columns), jnp.float32),
            pltpu.VMEM((half, mats, lines, width), jnp.float32),
            pltpu.VMEM((half, mats, lines, width), WIRE),
            pltpu.VMEM((half, mats, lines, width), WIRE),
            pltpu.VMEM((half, mats, lines, width), WIRE),
            pltpu.VMEM((half, mats, lines, width), WIRE),
            pltpu.VMEM((mats, lines, width), jnp.float32),
            pltpu.VMEM((3, mats, lines, width), jnp.float32),
            dma((n,)),
            dma((n,)),
            dma((half, mats)),
            dma((half, mats)),
            dma((half, mats)),
            dma((half, mats)),
            dma((half, mats)),
            dma((n, mats)),
            dma((half, mats)),
        ],
        compiler_params=pltpu.CompilerParams(
            collective_id=0, has_side_effects=True, vmem_limit_bytes=60 * 2**20
        ),
    )(
        gradients.transpose(0, 2, 1, 3), token_counts, modality, loss_weight,
        master.transpose(1, 0, 2), moment_one.transpose(1, 0, 2), moment_two.transpose(1, 0, 2),
    )
    return tuple(a.transpose(1, 0, 2) for a in (weights_new, first_new, second_new, working))


def solution(mesh):
    placed = (
        P("dp", None, None, "tensor"),
        P("dp", None),
        P("dp"),
        P(),
        P("dp", None, "tensor"),
        P("dp", None, "tensor"),
        P("dp", None, "tensor"),
    )
    return jax.shard_map(
        functools.partial(local, mesh.shape["dp"]),
        mesh=mesh,
        in_specs=placed,
        out_specs=(
            P("dp", None, "tensor"),
            P("dp", None, "tensor"),
            P("dp", None, "tensor"),
            P(None, None, "tensor"),
        ),
        check_vma=False,
    )
```

```python
import functools

import jax
import jax.numpy as jnp
from jax import lax
from jax.experimental import pallas as pl
from jax.experimental.pallas import tpu as pltpu
from jax.sharding import PartitionSpec as P

beta_one = 0.9
beta_two = 0.95
bias_one = 1.0 - 0.9**10
bias_two = 1.0 - 0.95**10
epsilon = 1e-08
learn_rate = 0.01
decay_rate = 0.1

WIRE = jnp.float32


def adam_update(grad_sum, first, second, weights):
    first_new = beta_one * first + (1.0 - beta_one) * grad_sum
    second_new = beta_two * second + (1.0 - beta_two) * grad_sum * grad_sum
    step_size = first_new / bias_one / (jnp.sqrt(second_new / bias_two) + epsilon)
    weights_new = weights - learn_rate * (step_size + decay_rate * weights)
    return (weights_new, first_new, second_new)


def kernel(
    n, rows_dev, mats, pieces, width,
    g_ref, counts_ref, modality_ref, weight_ref, master_ref, one_ref, two_ref,
    master_out, one_out, two_out, working,
    info_send, info, gathered, spread_out, kept, send_a, recv_a, send_b, recv_b, own, state,
    si, ri, sa, ra, sb, rb, sc, rc, sd,
):
    half = n // 2
    me = lax.axis_index("dp")
    o, i = me // 2, me % 2
    mate = 2 * o + (1 - i)

    barrier = pltpu.get_barrier_semaphore()

    def greet(k, _):
        pl.semaphore_signal(
            barrier, inc=1, device_id={"dp": (me + k) % n}, device_id_type=pl.DeviceIdType.MESH
        )
        return 0

    lax.fori_loop(1, n, greet, 0)

    def pack(src, dst, first_row, m):
        for r in range(rows_dev):
            for p in range(pieces):
                row = r * pieces + p
                dst[row : row + 1, :] = src[m, pl.ds(first_row + r, 1), p * width : (p + 1) * width]

    def remote(src, dst, send, recv, target):
        return pltpu.make_async_remote_copy(
            src_ref=src,
            dst_ref=dst,
            send_sem=send,
            recv_sem=recv,
            device_id={"dp": target},
            device_id_type=pl.DeviceIdType.MESH,
        )

    g = g_ref.at[0]

    line = lax.broadcasted_iota(jnp.int32, info_send.shape, 0)
    told = jnp.where(line == 3, modality_ref[0], 0)
    for m in range(3):
        told = jnp.where(line == m, counts_ref[0, m], told)
    info_send[...] = told
    info[me] = told

    def copy_a(od, m):
        return remote(send_a.at[od, m], recv_a.at[od, m], sa.at[od, m], ra.at[od, m], mate)

    def fill_a(k, m):
        od = (o + 1 + k) % half
        d = 2 * od + (1 - i)
        pack(g, send_a.at[od, m], d * rows_dev, m)

    fill_a(0, 0)
    pl.semaphore_wait(barrier, n - 1)
    copy_a((o + 1) % half, 0).start()

    def tell(k, _):
        remote(info_send, info.at[me], si.at[k], ri.at[me], (me + k) % n).start()
        return 0

    lax.fori_loop(1, n, tell, 0)

    for m in range(mats):
        def step_a(k, _, m=m):
            fill_a(k, m)
            copy_a((o + 1 + k) % half, m).start()
            return 0

        lax.fori_loop(1 if m == 0 else 0, half, step_a, 0)

    for m in range(mats):
        def keep(od, _, m=m):
            pack(g, kept.at[od, m], (2 * od + i) * rows_dev, m)
            return 0

        lax.fori_loop(0, half, keep, 0)
        pack(master_ref, state.at[0, m], 0, m)
        pack(one_ref, state.at[1, m], 0, m)
        pack(two_ref, state.at[2, m], 0, m)

    def hear(k, _):
        source = (me + k) % n
        remote(info_send, info.at[source], si.at[k], ri.at[source], source).wait()
        return 0

    lax.fori_loop(1, n, hear, 0)

    totals = lax.fori_loop(1, n, lambda r, t: t + info[r], info[0])
    ratios = [weight_ref[m] / totals[m : m + 1].astype(jnp.float32) for m in range(3)]

    def scale_of(replica):
        kind = info[replica][3:4]
        picked = jnp.where(kind == 2, ratios[2], jnp.where(kind == 1, ratios[1], ratios[0]))
        return jnp.concatenate([picked] * (width // 128), axis=1)

    my_scale = scale_of(me)
    mate_scale = scale_of(mate)

    def copy_b(od, m):
        return remote(send_b.at[od, m], recv_b.at[o, m], sb.at[od, m], rb.at[o, m], 2 * od + i)

    def paired(od, m):
        copy_a(od, m).wait()
        return kept[od, m] * my_scale + recv_a[od, m] * mate_scale

    def phase_b(m):
        def step(k, _):
            od = (o + 1 + k) % half
            send_b[od, m] = paired(od, m)
            copy_b(od, m).start()
            return 0

        lax.fori_loop(0, half - 1, step, 0)
        own[m] = paired(o, m)

    def copy_c(target, slot, m):
        return remote(gathered.at[me, m], gathered.at[me, m], sc.at[slot, m], rc.at[me, m], target)

    def finish(m):
        def add(k, total):
            source = (o + k) % half
            pltpu.make_async_remote_copy(
                src_ref=send_b.at[source, m], dst_ref=recv_b.at[source, m],
                send_sem=sb.at[source, m], recv_sem=rb.at[source, m],
                device_id={"dp": mate}, device_id_type=pl.DeviceIdType.MESH,
            ).wait()
            return total + recv_b[source, m]

        summed = lax.fori_loop(1, half, add, own[m])
        weights_new, first_new, second_new = adam_update(summed, state[1, m], state[2, m], state[0, m])
        gathered[me, m] = weights_new.astype(jnp.bfloat16)
        copy_c(mate, 0, m).start()

        def spread(k, _):
            copy_c(2 * ((o + k) % half) + i, k, m).start()
            return 0

        lax.fori_loop(1, half, spread, 0)
        state[0, m] = weights_new
        state[1, m] = first_new
        state[2, m] = second_new

    def write_state(m):
        for slot, out in enumerate((master_out, one_out, two_out)):
            for r in range(rows_dev):
                for p in range(pieces):
                    row = r * pieces + p
                    out[m, r : r + 1, p * width : (p + 1) * width] = state[slot, m, row : row + 1, :]

    def copy_d(od, m):
        d = 2 * od + i
        return remote(gathered.at[d, m], gathered.at[d, m], sd.at[od, m], rc.at[d, m], mate)

    def forward(m):
        def step(k, _):
            od = (o + k) % half
            d = 2 * od + i
            remote(gathered.at[d, m], gathered.at[d, m], sd.at[od, m], rc.at[d, m], mate).wait_recv()
            copy_d(od, m).start()
            return 0

        lax.fori_loop(1, half, step, 0)

    def unpack(d, m):
        block = gathered[d, m].astype(jnp.float32)
        for r in range(rows_dev):
            for p in range(pieces):
                row = r * pieces + p
                spread_out[pl.ds(d * rows_dev + r, 1), p * width : (p + 1) * width] = block[row : row + 1, :]

    def collect(m):
        def held(od, _):
            unpack(2 * od + i, m)
            return 0

        lax.fori_loop(0, half, held, 0)

        def last(k, _):
            od = (o + k) % half
            d = 2 * od + (1 - i)
            remote(gathered.at[d, m], gathered.at[d, m], sd.at[od, m], rc.at[d, m], mate).wait_recv()
            unpack(d, m)
            return 0

        lax.fori_loop(0, half, last, 0)
        working[m] = spread_out[...].astype(jnp.bfloat16)

    phase_b(0)
    for m in range(mats):
        if m + 1 < mats:
            phase_b(m + 1)
        finish(m)
        if m > 0:
            forward(m - 1)
    forward(mats - 1)
    for m in range(mats):
        write_state(m)
    for m in range(mats):
        collect(m)

    for m in range(mats):
        def given(k, _, m=m):
            copy_c(mate, k, m).wait_send()
            return 0

        lax.fori_loop(0, half, given, 0)

        def sent(k, _, m=m):
            copy_d((o + k) % half, m).wait_send()
            return 0

        lax.fori_loop(1, half, sent, 0)


def settle(count, mats, *refs):
    sources, targets, sems = refs[:count], refs[count : 2 * count], refs[-1]
    copies = [
        pltpu.make_async_copy(source.at[m], target.at[m], sems.at[k, m])
        for k, (source, target) in enumerate(zip(sources, targets))
        for m in range(mats)
    ]
    for copy in copies:
        copy.start()
    for copy in copies:
        copy.wait()


def local(n, gradients, token_counts, modality, loss_weight, master, moment_one, moment_two):
    rows_dev, mats, columns = master.shape
    half = n // 2
    pieces = 8
    width = columns // pieces
    lines = rows_dev * pieces
    vmem = pl.BlockSpec(memory_space=pltpu.VMEM)
    smem = pl.BlockSpec(memory_space=pltpu.SMEM)
    dma = pltpu.SemaphoreType.DMA
    state_shape = jax.ShapeDtypeStruct((mats, rows_dev, columns), jnp.float32)
    weights_new, first_new, second_new, working = pl.pallas_call(
        functools.partial(kernel, n, rows_dev, mats, pieces, width),
        out_shape=(
            state_shape,
            state_shape,
            state_shape,
            jax.ShapeDtypeStruct((mats, n * rows_dev, columns), jnp.bfloat16),
        ),
        in_specs=[vmem, smem, smem, smem, vmem, vmem, vmem],
        out_specs=(vmem,) * 4,
        scratch_shapes=[
            pltpu.VMEM((8, 128), jnp.int32),
            pltpu.VMEM((n, 8, 128), jnp.int32),
            pltpu.VMEM((n, mats, lines, width), jnp.bfloat16),
            pltpu.VMEM((n * rows_dev, columns), jnp.float32),
            pltpu.VMEM((half, mats, lines, width), jnp.float32),
            pltpu.VMEM((half, mats, lines, width), WIRE),
            pltpu.VMEM((half, mats, lines, width), WIRE),
            pltpu.VMEM((half, mats, lines, width), WIRE),
            pltpu.VMEM((half, mats, lines, width), WIRE),
            pltpu.VMEM((mats, lines, width), jnp.float32),
            pltpu.VMEM((3, mats, lines, width), jnp.float32),
            dma((n,)),
            dma((n,)),
            dma((half, mats)),
            dma((half, mats)),
            dma((half, mats)),
            dma((half, mats)),
            dma((half, mats)),
            dma((n, mats)),
            dma((half, mats)),
        ],
        compiler_params=pltpu.CompilerParams(
            collective_id=0, has_side_effects=True, vmem_limit_bytes=60 * 2**20
        ),
    )(
        gradients.transpose(0, 2, 1, 3), token_counts, modality, loss_weight,
        master.transpose(1, 0, 2), moment_one.transpose(1, 0, 2), moment_two.transpose(1, 0, 2),
    )
    results = (weights_new, first_new, second_new, working)
    count = len(results)
    anywhere = pl.BlockSpec(memory_space=pl.ANY)
    settled = pl.pallas_call(
        functools.partial(settle, count, mats),
        out_shape=tuple(jax.ShapeDtypeStruct(a.shape, a.dtype) for a in results),
        in_specs=[anywhere] * count,
        out_specs=(anywhere,) * count,
        scratch_shapes=[dma((count, mats))],
    )(*results)
    return tuple(a.transpose(1, 0, 2) for a in settled)


def solution(mesh):
    placed = (
        P("dp", None, None, "tensor"),
        P("dp", None),
        P("dp"),
        P(),
        P("dp", None, "tensor"),
        P("dp", None, "tensor"),
        P("dp", None, "tensor"),
    )
    return jax.shard_map(
        functools.partial(local, mesh.shape["dp"]),
        mesh=mesh,
        in_specs=placed,
        out_specs=(
            P("dp", None, "tensor"),
            P("dp", None, "tensor"),
            P("dp", None, "tensor"),
            P(None, None, "tensor"),
        ),
        check_vma=False,
    )
```

```python
import functools

import jax
import jax.numpy as jnp
from jax import lax
from jax.experimental import pallas as pl
from jax.experimental.pallas import tpu as pltpu
from jax.sharding import PartitionSpec as P

beta_one = 0.9
beta_two = 0.95
bias_one = 1.0 - 0.9**10
bias_two = 1.0 - 0.95**10
epsilon = 1e-08
learn_rate = 0.01
decay_rate = 0.1

WIRE = jnp.float32


def adam_update(grad_sum, first, second, weights):
    first_new = beta_one * first + (1.0 - beta_one) * grad_sum
    second_new = beta_two * second + (1.0 - beta_two) * grad_sum * grad_sum
    step_size = first_new / bias_one / (jnp.sqrt(second_new / bias_two) + epsilon)
    weights_new = weights - learn_rate * (step_size + decay_rate * weights)
    return (weights_new, first_new, second_new)


def kernel(
    n, rows_dev, mats, pieces, width,
    g_ref, counts_ref, modality_ref, weight_ref, master_ref, one_ref, two_ref,
    master_out, one_out, two_out, working,
    info_send, info, gathered, spread_out, kept, send_a, recv_a, send_b, recv_b, own, state,
    si, ri, sa, ra, sb, rb, sc, rc, sd,
):
    half = n // 2
    me = lax.axis_index("dp")
    o, i = me // 2, me % 2
    mate = 2 * o + (1 - i)

    barrier = pltpu.get_barrier_semaphore()

    def greet(k, _):
        pl.semaphore_signal(
            barrier, inc=1, device_id={"dp": (me + k) % n}, device_id_type=pl.DeviceIdType.MESH
        )
        return 0

    lax.fori_loop(1, n, greet, 0)

    def pack(src, dst, first_row, m):
        for r in range(rows_dev):
            for p in range(pieces):
                row = r * pieces + p
                dst[row : row + 1, :] = src[m, pl.ds(first_row + r, 1), p * width : (p + 1) * width]

    def remote(src, dst, send, recv, target):
        return pltpu.make_async_remote_copy(
            src_ref=src,
            dst_ref=dst,
            send_sem=send,
            recv_sem=recv,
            device_id={"dp": target},
            device_id_type=pl.DeviceIdType.MESH,
        )

    g = g_ref.at[0]

    line = lax.broadcasted_iota(jnp.int32, info_send.shape, 0)
    told = jnp.where(line == 3, modality_ref[0], 0)
    for m in range(3):
        told = jnp.where(line == m, counts_ref[0, m], told)
    info_send[...] = told
    info[me] = told

    def copy_a(od, m):
        return remote(send_a.at[od, m], recv_a.at[od, m], sa.at[od, m], ra.at[od, m], mate)

    def fill_a(k, m):
        od = (o + 1 + k) % half
        d = 2 * od + (1 - i)
        pack(g, send_a.at[od, m], d * rows_dev, m)

    fill_a(0, 0)
    pl.semaphore_wait(barrier, n - 1)
    copy_a((o + 1) % half, 0).start()

    def tell(k, _):
        remote(info_send, info.at[me], si.at[k], ri.at[me], (me + k) % n).start()
        return 0

    lax.fori_loop(1, n, tell, 0)

    for m in range(mats):
        def step_a(k, _, m=m):
            fill_a(k, m)
            copy_a((o + 1 + k) % half, m).start()
            return 0

        lax.fori_loop(1 if m == 0 else 0, half, step_a, 0)

    for m in range(mats):
        def keep(od, _, m=m):
            pack(g, kept.at[od, m], (2 * od + i) * rows_dev, m)
            return 0

        lax.fori_loop(0, half, keep, 0)
        pack(master_ref, state.at[0, m], 0, m)
        pack(one_ref, state.at[1, m], 0, m)
        pack(two_ref, state.at[2, m], 0, m)

    def hear(k, _):
        source = (me + k) % n
        remote(info_send, info.at[source], si.at[k], ri.at[source], source).wait()
        return 0

    lax.fori_loop(1, n, hear, 0)

    totals = lax.fori_loop(1, n, lambda r, t: t + info[r], info[0])
    ratios = [weight_ref[m] / totals[m : m + 1].astype(jnp.float32) for m in range(3)]

    def scale_of(replica):
        kind = info[replica][3:4]
        picked = jnp.where(kind == 2, ratios[2], jnp.where(kind == 1, ratios[1], ratios[0]))
        return jnp.concatenate([picked] * (width // 128), axis=1)

    my_scale = scale_of(me)
    mate_scale = scale_of(mate)

    def copy_b(od, m):
        return remote(send_b.at[od, m], recv_b.at[o, m], sb.at[od, m], rb.at[o, m], 2 * od + i)

    def paired(od, m):
        copy_a(od, m).wait()
        return kept[od, m] * my_scale + recv_a[od, m] * mate_scale

    def phase_b(m):
        def step(k, _):
            od = (o + 1 + k) % half
            send_b[od, m] = paired(od, m)
            copy_b(od, m).start()
            return 0

        lax.fori_loop(0, half - 1, step, 0)
        own[m] = paired(o, m)

    def copy_c(target, slot, m):
        return remote(gathered.at[me, m], gathered.at[me, m], sc.at[slot, m], rc.at[me, m], target)

    def finish(m):
        def add(k, total):
            source = (o + k) % half
            pltpu.make_async_remote_copy(
                src_ref=send_b.at[source, m], dst_ref=recv_b.at[source, m],
                send_sem=sb.at[source, m], recv_sem=rb.at[source, m],
                device_id={"dp": mate}, device_id_type=pl.DeviceIdType.MESH,
            ).wait()
            return total + recv_b[source, m]

        summed = lax.fori_loop(1, half, add, own[m])
        weights_new, first_new, second_new = adam_update(summed, state[1, m], state[2, m], state[0, m])
        gathered[me, m] = weights_new.astype(jnp.bfloat16)
        copy_c(mate, 0, m).start()

        def spread(k, _):
            copy_c(2 * ((o + k) % half) + i, k, m).start()
            return 0

        lax.fori_loop(1, half, spread, 0)
        state[0, m] = weights_new
        state[1, m] = first_new
        state[2, m] = second_new

    def write_state(m):
        for slot, out in enumerate((master_out, one_out, two_out)):
            for r in range(rows_dev):
                for p in range(pieces):
                    row = r * pieces + p
                    out[m, r : r + 1, p * width : (p + 1) * width] = state[slot, m, row : row + 1, :]

    def copy_d(od, m):
        d = 2 * od + i
        return remote(gathered.at[d, m], gathered.at[d, m], sd.at[od, m], rc.at[d, m], mate)

    def forward(m):
        def step(k, _):
            od = (o + k) % half
            d = 2 * od + i
            remote(gathered.at[d, m], gathered.at[d, m], sd.at[od, m], rc.at[d, m], mate).wait_recv()
            copy_d(od, m).start()
            return 0

        lax.fori_loop(1, half, step, 0)

    def unpack(d, m):
        block = gathered[d, m].astype(jnp.float32)
        for r in range(rows_dev):
            for p in range(pieces):
                row = r * pieces + p
                spread_out[pl.ds(d * rows_dev + r, 1), p * width : (p + 1) * width] = block[row : row + 1, :]

    def collect(m):
        def held(od, _):
            unpack(2 * od + i, m)
            return 0

        lax.fori_loop(0, half, held, 0)

        def last(k, _):
            od = (o + k) % half
            d = 2 * od + (1 - i)
            remote(gathered.at[d, m], gathered.at[d, m], sd.at[od, m], rc.at[d, m], mate).wait_recv()
            unpack(d, m)
            return 0

        lax.fori_loop(0, half, last, 0)
        working[m] = spread_out[...].astype(jnp.bfloat16)

    phase_b(0)
    for m in range(mats):
        if m + 1 < mats:
            phase_b(m + 1)
        finish(m)
        if m > 0:
            forward(m - 1)
    forward(mats - 1)
    for m in range(mats):
        write_state(m)
    for m in range(mats):
        collect(m)

    for m in range(mats):
        def given(k, _, m=m):
            copy_c(mate, k, m).wait_send()
            return 0

        lax.fori_loop(0, half, given, 0)

        def sent(k, _, m=m):
            copy_d((o + k) % half, m).wait_send()
            return 0

        lax.fori_loop(1, half, sent, 0)


def settle(count, mats, *refs):
    for source, target in zip(refs[:count], refs[count:]):
        for m in range(mats):
            target[m] = source[m]


def local(n, gradients, token_counts, modality, loss_weight, master, moment_one, moment_two):
    rows_dev, mats, columns = master.shape
    half = n // 2
    pieces = 8
    width = columns // pieces
    lines = rows_dev * pieces
    vmem = pl.BlockSpec(memory_space=pltpu.VMEM)
    smem = pl.BlockSpec(memory_space=pltpu.SMEM)
    dma = pltpu.SemaphoreType.DMA
    state_shape = jax.ShapeDtypeStruct((mats, rows_dev, columns), jnp.float32)
    weights_new, first_new, second_new, working = pl.pallas_call(
        functools.partial(kernel, n, rows_dev, mats, pieces, width),
        out_shape=(
            state_shape,
            state_shape,
            state_shape,
            jax.ShapeDtypeStruct((mats, n * rows_dev, columns), jnp.bfloat16),
        ),
        in_specs=[vmem, smem, smem, smem, vmem, vmem, vmem],
        out_specs=(vmem,) * 4,
        scratch_shapes=[
            pltpu.VMEM((8, 128), jnp.int32),
            pltpu.VMEM((n, 8, 128), jnp.int32),
            pltpu.VMEM((n, mats, lines, width), jnp.bfloat16),
            pltpu.VMEM((n * rows_dev, columns), jnp.float32),
            pltpu.VMEM((half, mats, lines, width), jnp.float32),
            pltpu.VMEM((half, mats, lines, width), WIRE),
            pltpu.VMEM((half, mats, lines, width), WIRE),
            pltpu.VMEM((half, mats, lines, width), WIRE),
            pltpu.VMEM((half, mats, lines, width), WIRE),
            pltpu.VMEM((mats, lines, width), jnp.float32),
            pltpu.VMEM((3, mats, lines, width), jnp.float32),
            dma((n,)),
            dma((n,)),
            dma((half, mats)),
            dma((half, mats)),
            dma((half, mats)),
            dma((half, mats)),
            dma((half, mats)),
            dma((n, mats)),
            dma((half, mats)),
        ],
        compiler_params=pltpu.CompilerParams(
            collective_id=0, has_side_effects=True, vmem_limit_bytes=60 * 2**20
        ),
    )(
        gradients.transpose(0, 2, 1, 3), token_counts, modality, loss_weight,
        master.transpose(1, 0, 2), moment_one.transpose(1, 0, 2), moment_two.transpose(1, 0, 2),
    )
    results = (weights_new, first_new, second_new, working)
    count = len(results)
    settled = pl.pallas_call(
        functools.partial(settle, count, mats),
        out_shape=tuple(jax.ShapeDtypeStruct(a.shape, a.dtype) for a in results),
        in_specs=[vmem] * count,
        out_specs=(vmem,) * count,
        compiler_params=pltpu.CompilerParams(vmem_limit_bytes=60 * 2**20),
    )(*results)
    return tuple(a.transpose(1, 0, 2) for a in settled)


def solution(mesh):
    placed = (
        P("dp", None, None, "tensor"),
        P("dp", None),
        P("dp"),
        P(),
        P("dp", None, "tensor"),
        P("dp", None, "tensor"),
        P("dp", None, "tensor"),
    )
    return jax.shard_map(
        functools.partial(local, mesh.shape["dp"]),
        mesh=mesh,
        in_specs=placed,
        out_specs=(
            P("dp", None, "tensor"),
            P("dp", None, "tensor"),
            P("dp", None, "tensor"),
            P(None, None, "tensor"),
        ),
        check_vma=False,
    )
```
